256 devices in a mesh: blk: 128 (over x, y_lo, z, core), rep: 2 (over y_hi).
Axes of the slice: x: 4, y: 4 (y_hi: 2, y_lo: 2; y = y_hi * 2 + y_lo), z: 8, core: 2. Of those that a mesh axis runs over, the one named last changes fastest.
Arguments:
- photo_vectors: bfloat16 [131072, 1152], P(('blk', 'rep')), may hold values from -3.6 to 3.6
- caption_vectors: bfloat16 [131072, 1152], P(('blk', 'rep')), may hold values from -3.6 to 3.6
- exponent_of_scale: float32 [1], replicated, may hold values from 1.609 to 2.708
- additive_intercept: float32 [1], replicated, may hold values from -3 to -1
Outputs:
- grad_images: bfloat16 [131072, 1152], P(('blk', 'rep'))
- grad_captions: bfloat16 [131072, 1152], P(('blk', 'rep'))
The draws below stay inside these ranges and needn't reach their ends.
All inputs are finite; a program needn't handle non-finite values.
Results may differ from the reference program's by a relative error of at most 0.009.
Values may be sent and summed in bfloat16 or wider, within the bound.
A program may use at most 128 MiB of HBM per device.

```python
import math
import jax
import jax.numpy as jnp
from jax import lax

D = 1152
TEXT_BLK = 1024
IMAGES = 131072
N_BLK = 128


def rough_scaling(key):
    key_rows, key_cols, key_noise = jax.random.split(key, 3)
    row_scale = jnp.exp(jax.random.uniform(key_rows, (IMAGES, 1), jnp.float32, 0.0, math.log(10.0)))
    col_scale = jnp.exp(jax.random.uniform(key_cols, (1, D), jnp.float32, 0.0, math.log(3.0)))
    return (key_noise, row_scale * col_scale * 0.03)


def shaped_rows(key):
    key_noise, scaling = rough_scaling(key)
    noise_part = jnp.clip(jax.random.normal(key_noise, (IMAGES, D), jnp.float32), -4.0, 4.0)
    return (noise_part * scaling).astype(jnp.bfloat16)


def draw_photo_vectors(key, part):
    key = jax.random.fold_in(key, 3)
    return shaped_rows(key)


def draw_caption_vectors(key, part):
    key = jax.random.fold_in(key, 5)
    return shaped_rows(key)


def setup_inputs(seed: int = 0) -> dict:
    key_of = jax.random.split(jax.random.key(seed), 5)
    return {
        "photo_vectors": draw_photo_vectors(jax.random.fold_in(key_of[4], 71), 0),
        "caption_vectors": draw_caption_vectors(jax.random.fold_in(key_of[4], 71), 0),
        "exponent_of_scale": jnp.clip(jax.random.uniform(key_of[2], (1,), jnp.float32, 1.609, 2.708), 1.609, 2.708),
        "additive_intercept": jnp.clip(jax.random.uniform(key_of[3], (1,), jnp.float32, -3.0, -1.0), -3.0, -1.0),
    }


def unit_rows(values):
    inverse = lax.rsqrt(lax.optimization_barrier(jnp.sum(values * values, axis=1, keepdims=True)) + 1e-06)
    return (values * inverse, inverse)

def back_rows(upstream, direction, inverse):
    return inverse * (upstream - direction * lax.optimization_barrier(jnp.sum(upstream * direction, axis=1, keepdims=True)))

def entry_coefficient(similarity_matrix, agreeing_couples, similarity_scale):
    target_polarity = jnp.where(agreeing_couples, 1.0, -1.0).astype(jnp.float32)
    return (similarity_scale * -target_polarity * jax.nn.sigmoid(-target_polarity * similarity_matrix)).astype(jnp.bfloat16)

def reference(photo_vectors, caption_vectors, exponent_of_scale, additive_intercept):
    image_dir, image_inverse = unit_rows(photo_vectors.astype(jnp.float32))
    caption_dir, caption_inverse = unit_rows(caption_vectors.astype(jnp.float32))
    image_unit = image_dir.astype(jnp.bfloat16)
    caption_unit = caption_dir.astype(jnp.bfloat16)
    similarity_scale = jnp.exp(exponent_of_scale[0])
    moved_intercept = additive_intercept[0]
    image_blocks = image_unit.reshape(N_BLK, TEXT_BLK, D)
    caption_blocks = caption_unit.reshape(N_BLK, TEXT_BLK, D)
    identity_mask = jnp.eye(TEXT_BLK, dtype=bool)
    negative_couples = jnp.zeros((TEXT_BLK, TEXT_BLK), dtype=bool)

    def visit(caption_acc, block_id):
        photo_slice_entries = lax.dynamic_index_in_dim(image_blocks, block_id, 0, keepdims=False)
        image_grad = jnp.zeros((TEXT_BLK, D), jnp.float32)
        for neighbour_distance in (-1, 0, 1):
            other_id = ((block_id + neighbour_distance) % N_BLK).astype(jnp.int32)
            caption_slice_entries = lax.dynamic_index_in_dim(caption_blocks, other_id, 0, keepdims=False)
            similarity_matrix = similarity_scale * jnp.einsum('dn,ln->dl', photo_slice_entries, caption_slice_entries, preferred_element_type=jnp.float32) + moved_intercept
            logistic_factor = entry_coefficient(similarity_matrix, identity_mask if neighbour_distance == 0 else negative_couples, similarity_scale)
            image_grad = image_grad + jnp.einsum('ij,jd->id', logistic_factor, caption_slice_entries, preferred_element_type=jnp.float32)
            update = jnp.einsum('ij,id->jd', logistic_factor, photo_slice_entries, preferred_element_type=jnp.float32)
            current = lax.dynamic_index_in_dim(caption_acc, other_id, 0, keepdims=False)
            caption_acc = lax.dynamic_update_index_in_dim(caption_acc, current + update, other_id, 0)
        return (caption_acc, image_grad)
    caption_acc, image_grads = lax.scan(visit, jnp.zeros((N_BLK, TEXT_BLK, D), jnp.float32), jnp.arange(N_BLK, dtype=jnp.int32))
    grad_images = back_rows(image_grads.reshape(IMAGES, D), image_dir, image_inverse).astype(jnp.bfloat16)
    grad_captions = back_rows(caption_acc.reshape(IMAGES, D), caption_dir, caption_inverse).astype(jnp.bfloat16)
    return (grad_images, grad_captions)
```

```python
import functools

import jax
import jax.numpy as jnp
from jax import lax
from jax.experimental import pallas as pl
from jax.experimental.pallas import tpu as pltpu
from jax.sharding import PartitionSpec as P

MESH = pl.DeviceIdType.MESH
PIECES = 8
SHIFTED = 0
AHEAD = 8
OUT_NEAR, REP, IN_FAR, OUT_FAR = range(4)


def kernel(
    n_blk, n_z, exp_ref, icpt_ref, img_hbm, cap_hbm, gi_hbm, gc_hbm,
    raw, inv, own, pdir, win, acc, res,
    raw_sem, out_sem, win_recv, pdir_recv, rep_send, out_send, in_send, fin_send, fout_send, e_send, e2_send,
):
    rows, width = own.shape[1], own.shape[2]
    pr = rows // PIECES
    blk, rep = lax.axis_index("blk"), lax.axis_index("rep")
    core = lax.rem(blk, 2)
    z = lax.rem(blk // 2, n_z)
    away = 2 * core - 1
    outer = lax.rem(blk + away + n_blk, n_blk)
    inner = blk - away
    z_end = core * (n_z - 1)
    edge = z == z_end
    behind = (core == 0) & (z == n_z - 1) | (core == 1) & (z == 0)
    beside = (core == 1) & (z == n_z - 2) | (core == 0) & (z == 1)
    rep_id = {"blk": blk, "rep": 1 - rep}
    inner_id = {"blk": inner, "rep": rep}
    outer_id = {"blk": outer, "rep": rep}
    cross_id = {"blk": outer, "rep": 1 - rep}

    def rows_of(j):
        return pl.ds(pl.multiple_of(j * pr, pr), pr)

    def load(j):
        return (
            pltpu.make_async_copy(cap_hbm.at[rows_of(j)], raw.at[0, rows_of(j)], raw_sem.at[0, j]),
            pltpu.make_async_copy(img_hbm.at[rows_of(j)], raw.at[1, rows_of(j)], raw_sem.at[1, j]),
        )

    def slot(place, j):
        return win.at[j, :, pl.ds(place * pr, pr)]

    def remote(src, dst, send, recv, target):
        return pltpu.make_async_remote_copy(
            src_ref=src, dst_ref=dst, send_sem=send, recv_sem=recv, device_id=target, device_id_type=MESH
        )

    def mine(j):
        return own.at[:, rows_of(j)]

    def to_rep(j):
        return remote(mine(j), slot(REP, j), rep_send.at[j], win_recv.at[REP, j], rep_id)

    def to_outer(j):
        return remote(mine(j), slot(OUT_NEAR, j), out_send.at[j], win_recv.at[OUT_NEAR, j], outer_id)

    def to_inner(j):
        return remote(mine(j), pdir.at[:, rows_of(j)], in_send.at[j], pdir_recv.at[j], inner_id)

    def to_cross(j):
        return remote(mine(j), slot(OUT_FAR, j), fout_send.at[j], win_recv.at[OUT_FAR, j], cross_id)

    def pass_inner(j):
        return remote(slot(REP, j), slot(IN_FAR, j), fin_send.at[j], win_recv.at[IN_FAR, j], inner_id)

    def pass_outer(j):
        return remote(slot(REP, j), slot(OUT_FAR, j), fout_send.at[j], win_recv.at[OUT_FAR, j], outer_id)

    def pass_rep(j):
        return remote(slot(OUT_NEAR, j), slot(OUT_FAR, j), e_send.at[j], win_recv.at[OUT_FAR, j], rep_id)

    def pass_back(j):
        return remote(slot(OUT_FAR, j), slot(REP, j), e2_send.at[j], win_recv.at[REP, j], outer_id)

    def got(place, j):
        pltpu.make_async_copy(slot(place, j), slot(place, j), win_recv.at[place, j]).wait()

    def each(count, body):
        lax.fori_loop(0, count, lambda j, c: (body(j), c)[1], 0)

    each(PIECES, lambda j: [c.start() for c in load(j)])

    barrier = pltpu.get_barrier_semaphore()
    for target in (rep_id, inner_id, outer_id, cross_id):
        pl.semaphore_signal(barrier, inc=1, device_id=target, device_id_type=MESH)
    pl.semaphore_wait(barrier, 4)

    def send_mine(j):
        @pl.when(jnp.logical_not(behind & (j < SHIFTED)))
        def _():
            to_rep(j).start()

        to_outer(j).start()
        to_inner(j).start()

        @pl.when(edge)
        def _():
            to_cross(j).start()

    def prepare(j):
        for c in load(j):
            c.wait()
        for a in range(2):
            values = raw[a, rows_of(j), :].astype(jnp.float32)
            inverse = lax.rsqrt(jnp.sum(values * values, axis=1, keepdims=True) + 1e-06)
            own[a, rows_of(j), :] = (values * inverse).astype(jnp.bfloat16)
            inv[a, rows_of(j), :] = inverse

        @pl.when(j < AHEAD)
        def _():
            send_mine(j)

    each(PIECES, prepare)

    scale = jnp.exp(exp_ref[...])
    icpt = icpt_ref[...]

    def weights(side, others, diagonal):
        product = lax.dot_general(
            own[side], others, (((1,), (1,)), ((), ())), preferred_element_type=jnp.float32
        )
        logits = scale * product + icpt
        if diagonal is None:
            factor = scale / (1.0 + jnp.exp(-logits))
        else:
            row = lax.broadcasted_iota(jnp.int32, product.shape, 0)
            col = lax.broadcasted_iota(jnp.int32, product.shape, 1) + diagonal
            agree = row == col
            factor = jnp.where(agree, -scale, scale) / (1.0 + jnp.exp(jnp.where(agree, logits, -logits)))
        return factor.astype(jnp.bfloat16)

    def step(caps, imgs, diagonal=None, first=False):
        for side, others in ((1, caps), (0, imgs)):
            term = lax.dot_general(
                weights(side, others, diagonal), others, (((1,), (0,)), ((), ())),
                preferred_element_type=jnp.float32,
            )
            acc[side] = term if first else acc[side] + term

    half = rows // 2
    step(own[0, :half], own[1, :half], 0, True)
    step(own[0, half:], own[1, half:], half)

    each(PIECES, lambda j: pltpu.make_async_copy(
        pdir.at[:, rows_of(j)], pdir.at[:, rows_of(j)], pdir_recv.at[j]).wait())

    def inner_step(k):
        at = pl.ds(pl.multiple_of(k * half, half), half)
        step(pdir[0, at, :], pdir[1, at, :])

    each(2, inner_step)

    def serve(j):
        got(REP, j)
        pass_inner(j).start()

        @pl.when(jnp.logical_not(edge | behind & (j < SHIFTED)))
        def _():
            pass_outer(j).start()

        got(OUT_NEAR, j)

        @pl.when(beside & (j < SHIFTED))
        def _():
            pass_rep(j).start()

        @pl.when(j + AHEAD < PIECES)
        def _():
            send_mine(j + AHEAD)

    def finish(j):
        got(OUT_FAR, j)

        @pl.when(beside & (j < SHIFTED))
        def _():
            pass_back(j).start()

        got(IN_FAR, j)
        step(win[j, 0], win[j, 1])

    serve(0)

    def body(j):
        @pl.when(j < PIECES)
        def _():
            serve(j)
        finish(j - 1)

    lax.fori_loop(1, PIECES + 1, lambda j, c: (body(j), c)[1], 0)

    def close(a, out):
        def part(j):
            direction = raw[a, rows_of(j), :].astype(jnp.float32) * inv[a, rows_of(j), :]
            upstream = acc[a, rows_of(j), :]
            along = jnp.sum(upstream * direction, axis=1, keepdims=True)
            res[a, rows_of(j), :] = (inv[a, rows_of(j), :] * (upstream - direction * along)).astype(jnp.bfloat16)
            pltpu.make_async_copy(res.at[a, rows_of(j)], out.at[rows_of(j)], out_sem.at[a, j]).start()
        each(PIECES, part)

    close(1, gi_hbm)
    close(0, gc_hbm)

    def drain(j):
        for a, out in ((1, gi_hbm), (0, gc_hbm)):
            pltpu.make_async_copy(res.at[a, rows_of(j)], out.at[rows_of(j)], out_sem.at[a, j]).wait()
        to_outer(j).wait_send()
        to_inner(j).wait_send()
        pass_inner(j).wait_send()

        @pl.when(jnp.logical_not(behind & (j < SHIFTED)))
        def _():
            to_rep(j).wait_send()

        @pl.when(edge)
        def _():
            to_cross(j).wait_send()

        @pl.when(jnp.logical_not(edge | behind & (j < SHIFTED)))
        def _():
            pass_outer(j).wait_send()

        @pl.when(beside & (j < SHIFTED))
        def _():
            pass_rep(j).wait_send()
            pass_back(j).wait_send()

    each(PIECES, drain)


def solution(mesh):
    n_blk = mesh.shape["blk"]

    def shards(photo_vectors, caption_vectors, exponent_of_scale, additive_intercept):
        rows, width = photo_vectors.shape
        pr = rows // PIECES
        bf16, f32 = jnp.bfloat16, jnp.float32
        dma = pltpu.SemaphoreType.DMA
        vmem = pl.BlockSpec(memory_space=pltpu.VMEM)
        anywhere = pl.BlockSpec(memory_space=pl.ANY)
        return pl.pallas_call(
            functools.partial(kernel, n_blk, 8),
            out_shape=[jax.ShapeDtypeStruct((rows, width), bf16)] * 2,
            in_specs=[vmem, vmem, anywhere, anywhere],
            out_specs=[anywhere] * 2,
            scratch_shapes=[
                pltpu.VMEM((2, rows, width), bf16),
                pltpu.VMEM((2, rows, 1), f32),
                pltpu.VMEM((2, rows, width), bf16),
                pltpu.VMEM((2, rows, width), bf16),
                pltpu.VMEM((PIECES, 2, 4 * pr, width), bf16),
                pltpu.VMEM((2, rows, width), f32),
                pltpu.VMEM((2, rows, width), bf16),
                dma((2, PIECES)),
                dma((2, PIECES)),
                dma((4, PIECES)),
            ] + [dma((PIECES,))] * 8,
            compiler_params=pltpu.CompilerParams(
                collective_id=0, has_side_effects=True, vmem_limit_bytes=56 * 1024 * 1024
            ),
            cost_estimate=pl.CostEstimate(
                flops=24 * 2 * rows * rows * width, bytes_accessed=8 * rows * width, transcendentals=12 * rows * rows
            ),
        )(
            exponent_of_scale.reshape(1, 1), additive_intercept.reshape(1, 1), photo_vectors, caption_vectors
        )

    whole = P(("blk", "rep"), None)
    return jax.shard_map(
        shards,
        mesh=mesh,
        in_specs=(whole, whole, P(), P()),
        out_specs=(whole, whole),
        check_vma=False,
    )
```

```python
import functools

import jax
import jax.numpy as jnp
from jax import lax
from jax.experimental import pallas as pl
from jax.experimental.pallas import tpu as pltpu
from jax.sharding import PartitionSpec as P

MESH = pl.DeviceIdType.MESH
PIECES = 8
SEND_AHEAD = 4
RELAY_AHEAD = 2
EXTRA = 0
OUT_NEAR, REP, IN_FAR, OUT_FAR = range(4)


def kernel(
    n_blk, n_z, exp_ref, icpt_ref, img_hbm, cap_hbm, gi_hbm, gc_hbm,
    raw, inv, own, pdir, win, relay, acc, res,
    raw_sem, out_sem, win_recv, pdir_recv, relay_recv,
    in_send, rep_send, out_send, fin_send, fout_send, near_send, far_send, cross_send,
):
    rows, width = own.shape[1], own.shape[2]
    pr = rows // PIECES
    blk, rep = lax.axis_index("blk"), lax.axis_index("rep")
    core = lax.rem(blk, 2)
    z = lax.rem(blk // 2, n_z)
    away = 2 * core - 1
    outer = lax.rem(blk + away + n_blk, n_blk)
    inner = blk - away
    edge = z == core * (n_z - 1)
    inside = jnp.logical_not(edge)
    pal = blk + 2 * n_z * (1 - 2 * lax.rem(blk // (2 * n_z), 2))
    beyond = lax.rem(pal + away + n_blk, n_blk)
    outer_low = lax.rem(outer // (2 * n_z), 2)
    source = outer + 2 * n_z * (1 - 2 * outer_low)
    rep_id = {"blk": blk, "rep": 1 - rep}
    inner_id = {"blk": inner, "rep": rep}
    outer_id = {"blk": outer, "rep": rep}
    near_id = {"blk": pal, "rep": rep}
    far_id = {"blk": pal, "rep": 1 - rep}
    beyond_id = {"blk": beyond, "rep": rep}
    source_id = {"blk": source, "rep": rep}

    def rows_of(j):
        return pl.ds(pl.multiple_of(j * pr, pr), pr)

    def load(j):
        return (
            pltpu.make_async_copy(cap_hbm.at[rows_of(j)], raw.at[0, rows_of(j)], raw_sem.at[0, j]),
            pltpu.make_async_copy(img_hbm.at[rows_of(j)], raw.at[1, rows_of(j)], raw_sem.at[1, j]),
        )

    def slot(place, j):
        return win.at[j, :, pl.ds(place * pr, pr)]

    def remote(src, dst, send, recv, target):
        return pltpu.make_async_remote_copy(
            src_ref=src, dst_ref=dst, send_sem=send, recv_sem=recv, device_id=target, device_id_type=MESH
        )

    def mine(j):
        return own.at[:, rows_of(j)]

    def to_rep(j):
        return remote(mine(j), slot(REP, j), rep_send.at[j], win_recv.at[REP, j], rep_id)

    def to_outer(j):
        return remote(mine(j), slot(OUT_NEAR, j), out_send.at[j], win_recv.at[OUT_NEAR, j], outer_id)

    def to_inner(j):
        return remote(mine(j), pdir.at[:, rows_of(j)], in_send.at[j], pdir_recv.at[j], inner_id)

    def to_near(j):
        return remote(mine(j), relay.at[0, :, rows_of(j)], rep_send.at[j], relay_recv.at[0, j], near_id)

    def to_far(j):
        return remote(mine(j), relay.at[1, :, rows_of(j)], out_send.at[j], relay_recv.at[1, j], far_id)

    def pass_inner(j):
        return remote(slot(REP, j), slot(IN_FAR, j), fin_send.at[j], win_recv.at[IN_FAR, j], inner_id)

    def pass_outer(j):
        return remote(slot(REP, j), slot(OUT_FAR, j), fout_send.at[j], win_recv.at[OUT_FAR, j], outer_id)

    def near_beyond(j):
        return remote(relay.at[0, :, rows_of(j)], slot(OUT_NEAR, j), near_send.at[j], win_recv.at[OUT_NEAR, j], beyond_id)

    def far_beyond(j):
        return remote(relay.at[1, :, rows_of(j)], slot(OUT_FAR, j), far_send.at[j], win_recv.at[OUT_FAR, j], beyond_id)

    def near_across(j):
        return remote(relay.at[0, :, rows_of(j)], slot(REP, j), cross_send.at[0, j], win_recv.at[REP, j], far_id)

    def far_across(j):
        return remote(relay.at[1, :, rows_of(j)], slot(REP, j), cross_send.at[1, j], win_recv.at[REP, j], near_id)

    def got(place, j):
        pltpu.make_async_copy(slot(place, j), slot(place, j), win_recv.at[place, j]).wait()

    def got_relay(side, j):
        at = relay.at[side, :, rows_of(j)]
        pltpu.make_async_copy(at, at, relay_recv.at[side, j]).wait()

    def each(count, body):
        lax.fori_loop(0, count, lambda j, c: (body(j), c)[1], 0)

    each(PIECES, lambda j: [c.start() for c in load(j)])

    barrier = pltpu.get_barrier_semaphore()

    def greet(*targets):
        for target in targets:
            pl.semaphore_signal(barrier, inc=1, device_id=target, device_id_type=MESH)

    greet(inner_id)

    @pl.when(inside)
    def _():
        greet(rep_id, outer_id)

    @pl.when(edge)
    def _():
        greet(near_id, far_id, beyond_id, source_id)

    def prepare(j):
        for c in load(j):
            c.wait()
        for a in range(2):
            values = raw[a, rows_of(j), :].astype(jnp.float32)
            inverse = lax.rsqrt(jnp.sum(values * values, axis=1, keepdims=True) + 1e-06)
            own[a, rows_of(j), :] = (values * inverse).astype(jnp.bfloat16)
            inv[a, rows_of(j), :] = inverse

    def send_first(j):
        @pl.when(inside)
        def _():
            to_rep(j).start()

        @pl.when(edge)
        def _():
            to_near(j).start()

    def send_second(j):
        @pl.when(inside)
        def _():
            to_outer(j).start()

        @pl.when(edge)
        def _():
            to_far(j).start()

    prepare(0)

    @pl.when(inside)
    def _():
        pl.semaphore_wait(barrier, 3)

    @pl.when(edge)
    def _():
        pl.semaphore_wait(barrier, 5)

    def begin(j):
        @pl.when(j > 0)
        def _():
            prepare(j)

        @pl.when(j < SEND_AHEAD)
        def _():
            send_first(j)
            send_second(j)

        to_inner(j).start()

    each(PIECES, begin)

    scale = jnp.exp(exp_ref[...])
    icpt = icpt_ref[...]

    def weights(side, others, diagonal):
        product = lax.dot_general(
            own[side], others, (((1,), (1,)), ((), ())), preferred_element_type=jnp.float32
        )
        logits = scale * product + icpt
        if diagonal is None:
            factor = scale / (1.0 + jnp.exp(-logits))
        else:
            row = lax.broadcasted_iota(jnp.int32, product.shape, 0)
            col = lax.broadcasted_iota(jnp.int32, product.shape, 1) + diagonal
            agree = row == col
            factor = jnp.where(agree, -scale, scale) / (1.0 + jnp.exp(jnp.where(agree, logits, -logits)))
        return factor.astype(jnp.bfloat16)

    def step(caps, imgs, diagonal=None, first=False):
        factors = [weights(1, caps, diagonal), weights(0, imgs, diagonal)]
        for side, others, factor in ((1, caps, factors[0]), (0, imgs, factors[1])):
            term = lax.dot_general(factor, others, (((1,), (0,)), ((), ())), preferred_element_type=jnp.float32)
            acc[side] = term if first else acc[side] + term

    def hand_on(j):
        @pl.when(edge)
        def _():
            turn = lax.rem(j, 2) == rep
            got_relay(0, j)

            @pl.when(turn)
            def _():
                near_across(j).start()

            near_beyond(j).start()
            got_relay(1, j)

            @pl.when(turn)
            def _():
                far_across(j).start()

            far_beyond(j).start()

    def serve(j):
        @pl.when(j + SEND_AHEAD < PIECES)
        def _():
            send_first(j + SEND_AHEAD)
            send_second(j + SEND_AHEAD)

        @pl.when(j + RELAY_AHEAD < PIECES)
        def _():
            hand_on(j + RELAY_AHEAD)

        got(REP, j)
        pass_inner(j).start()

        @pl.when(inside)
        def _():
            pass_outer(j).start()

    def finish(j):
        got(OUT_NEAR, j)
        got(OUT_FAR, j)
        got(IN_FAR, j)
        step(win[j, 0], win[j, 1])

    half = rows // 2
    for k in range(RELAY_AHEAD):
        hand_on(k)
        if k < 2:
            step(own[0, k * half:(k + 1) * half], own[1, k * half:(k + 1) * half], k * half, k == 0)

    each(PIECES, lambda j: pltpu.make_async_copy(
        pdir.at[:, rows_of(j)], pdir.at[:, rows_of(j)], pdir_recv.at[j]).wait())

    def body(j):
        @pl.when(j < PIECES)
        def _():
            serve(j)

        @pl.when(j < 2)
        def _():
            at = pl.ds(pl.multiple_of(j * half, half), half)
            step(pdir[0, at, :], pdir[1, at, :])

        @pl.when(j > 0)
        def _():
            finish(j - 1)

    each(PIECES + 1, body)
    each(EXTRA, lambda j: step(win[j, 0], win[j, 1]))

    def close(a, out):
        def part(j):
            direction = raw[a, rows_of(j), :].astype(jnp.float32) * inv[a, rows_of(j), :]
            upstream = acc[a, rows_of(j), :]
            along = jnp.sum(upstream * direction, axis=1, keepdims=True)
            res[a, rows_of(j), :] = (inv[a, rows_of(j), :] * (upstream - direction * along)).astype(jnp.bfloat16)
            pltpu.make_async_copy(res.at[a, rows_of(j)], out.at[rows_of(j)], out_sem.at[a, j]).start()
        each(PIECES, part)

    close(1, gi_hbm)
    close(0, gc_hbm)

    def drain(j):
        for a, out in ((1, gi_hbm), (0, gc_hbm)):
            pltpu.make_async_copy(res.at[a, rows_of(j)], out.at[rows_of(j)], out_sem.at[a, j]).wait()
        to_inner(j).wait_send()
        pass_inner(j).wait_send()

        @pl.when(inside)
        def _():
            to_rep(j).wait_send()
            to_outer(j).wait_send()
            pass_outer(j).wait_send()

        @pl.when(edge)
        def _():
            to_near(j).wait_send()
            to_far(j).wait_send()
            near_beyond(j).wait_send()
            far_beyond(j).wait_send()

            @pl.when(lax.rem(j, 2) == rep)
            def _():
                near_across(j).wait_send()
                far_across(j).wait_send()

    each(PIECES, drain)


def solution(mesh):
    n_blk = mesh.shape["blk"]

    def shards(photo_vectors, caption_vectors, exponent_of_scale, additive_intercept):
        rows, width = photo_vectors.shape
        pr = rows // PIECES
        bf16, f32 = jnp.bfloat16, jnp.float32
        dma = pltpu.SemaphoreType.DMA
        vmem = pl.BlockSpec(memory_space=pltpu.VMEM)
        anywhere = pl.BlockSpec(memory_space=pl.ANY)
        return pl.pallas_call(
            functools.partial(kernel, n_blk, 8),
            out_shape=[jax.ShapeDtypeStruct((rows, width), bf16)] * 2,
            in_specs=[vmem, vmem, anywhere, anywhere],
            out_specs=[anywhere] * 2,
            scratch_shapes=[
                pltpu.VMEM((2, rows, width), bf16),
                pltpu.VMEM((2, rows, 1), f32),
                pltpu.VMEM((2, rows, width), bf16),
                pltpu.VMEM((2, rows, width), bf16),
                pltpu.VMEM((PIECES, 2, 4 * pr, width), bf16),
                pltpu.VMEM((2, 2, rows, width), bf16),
                pltpu.VMEM((2, rows, width), f32),
                pltpu.VMEM((2, rows, width), bf16),
                dma((2, PIECES)),
                dma((2, PIECES)),
                dma((4, PIECES)),
                dma((PIECES,)),
                dma((2, PIECES)),
            ] + [dma((PIECES,))] * 7 + [dma((2, PIECES))],
            compiler_params=pltpu.CompilerParams(
                collective_id=0, has_side_effects=True, vmem_limit_bytes=56 * 1024 * 1024
            ),
            cost_estimate=pl.CostEstimate(
                flops=24 * 2 * rows * rows * width, bytes_accessed=8 * rows * width, transcendentals=12 * rows * rows
            ),
        )(
            exponent_of_scale.reshape(1, 1), additive_intercept.reshape(1, 1), photo_vectors, caption_vectors
        )

    whole = P(("blk", "rep"), None)
    return jax.shard_map(
        shards,
        mesh=mesh,
        in_specs=(whole, whole, P(), P()),
        out_specs=(whole, whole),
        check_vma=False,
    )
```

```python
import functools

import jax
import jax.numpy as jnp
from jax import lax
from jax.experimental import pallas as pl
from jax.experimental.pallas import tpu as pltpu
from jax.sharding import PartitionSpec as P

MESH = pl.DeviceIdType.MESH
PIECES = 8
SEND_AHEAD = 4
RELAY_AHEAD = 2
SHIFTED = 2
SHIFT_OUT = 1
SHIFT_BACK = 3
PREPARE = 2
CLOSE = 256
OUT_NEAR, REP, IN_FAR, OUT_FAR = range(4)


def kernel(
    n_blk, n_z, exp_ref, icpt_ref, img_hbm, cap_hbm, gi_hbm, gc_hbm,
    raw, inv, own, pdir, win, relay, acc, res,
    raw_sem, out_sem, win_recv, pdir_recv, relay_recv,
    in_send, rep_send, out_send, fin_send, fout_send, near_send, far_send, cross_send, shift_send, back_send,
):
    rows, width = own.shape[1], own.shape[2]
    pr = rows // PIECES
    blk, rep = lax.axis_index("blk"), lax.axis_index("rep")
    core = lax.rem(blk, 2)
    z = lax.rem(blk // 2, n_z)
    away = 2 * core - 1
    outer = lax.rem(blk + away + n_blk, n_blk)
    inner = blk - away
    edge = z == core * (n_z - 1)
    inside = jnp.logical_not(edge)
    behind = z == (1 - core) * (n_z - 1)
    beside = z == core * (n_z - 2) + (1 - core)
    pal = blk + 2 * n_z * (1 - 2 * lax.rem(blk // (2 * n_z), 2))
    beyond = lax.rem(pal + away + n_blk, n_blk)
    outer_low = lax.rem(outer // (2 * n_z), 2)
    source = outer + 2 * n_z * (1 - 2 * outer_low)
    rep_id = {"blk": blk, "rep": 1 - rep}
    inner_id = {"blk": inner, "rep": rep}
    outer_id = {"blk": outer, "rep": rep}
    near_id = {"blk": pal, "rep": rep}
    far_id = {"blk": pal, "rep": 1 - rep}
    beyond_id = {"blk": beyond, "rep": rep}
    source_id = {"blk": source, "rep": rep}

    def rows_of(j):
        return pl.ds(pl.multiple_of(j * pr, pr), pr)

    def load(j):
        return (
            pltpu.make_async_copy(cap_hbm.at[rows_of(j)], raw.at[0, rows_of(j)], raw_sem.at[0, j]),
            pltpu.make_async_copy(img_hbm.at[rows_of(j)], raw.at[1, rows_of(j)], raw_sem.at[1, j]),
        )

    def slot(place, j):
        return win.at[j, :, pl.ds(place * pr, pr)]

    def remote(src, dst, send, recv, target):
        return pltpu.make_async_remote_copy(
            src_ref=src, dst_ref=dst, send_sem=send, recv_sem=recv, device_id=target, device_id_type=MESH
        )

    def mine(j):
        return own.at[:, rows_of(j)]

    def to_rep(j):
        return remote(mine(j), slot(REP, j), rep_send.at[j], win_recv.at[REP, j], rep_id)

    def to_outer(j):
        return remote(mine(j), slot(OUT_NEAR, j), out_send.at[j], win_recv.at[OUT_NEAR, j], outer_id)

    def to_inner(j):
        return remote(mine(j), pdir.at[:, rows_of(j)], in_send.at[j], pdir_recv.at[j], inner_id)

    def to_near(j):
        return remote(mine(j), relay.at[0, :, rows_of(j)], rep_send.at[j], relay_recv.at[0, j], near_id)

    def to_far(j):
        return remote(mine(j), relay.at[1, :, rows_of(j)], out_send.at[j], relay_recv.at[1, j], far_id)

    def pass_inner(j):
        return remote(slot(REP, j), slot(IN_FAR, j), fin_send.at[j], win_recv.at[IN_FAR, j], inner_id)

    def pass_outer(j):
        return remote(slot(REP, j), slot(OUT_FAR, j), fout_send.at[j], win_recv.at[OUT_FAR, j], outer_id)

    def shift_rep(j):
        return remote(slot(OUT_NEAR, j), slot(OUT_FAR, j), shift_send.at[j], win_recv.at[OUT_FAR, j], rep_id)

    def shift_back(j):
        return remote(slot(OUT_FAR, j), slot(REP, j), back_send.at[j], win_recv.at[REP, j], outer_id)

    def near_beyond(j):
        return remote(relay.at[0, :, rows_of(j)], slot(OUT_NEAR, j), near_send.at[j], win_recv.at[OUT_NEAR, j], beyond_id)

    def far_beyond(j):
        return remote(relay.at[1, :, rows_of(j)], slot(OUT_FAR, j), far_send.at[j], win_recv.at[OUT_FAR, j], beyond_id)

    def near_across(j):
        return remote(relay.at[0, :, rows_of(j)], slot(REP, j), cross_send.at[0, j], win_recv.at[REP, j], far_id)

    def far_across(j):
        return remote(relay.at[1, :, rows_of(j)], slot(REP, j), cross_send.at[1, j], win_recv.at[REP, j], near_id)

    def got(place, j):
        pltpu.make_async_copy(slot(place, j), slot(place, j), win_recv.at[place, j]).wait()

    def got_relay(side, j):
        at = relay.at[side, :, rows_of(j)]
        pltpu.make_async_copy(at, at, relay_recv.at[side, j]).wait()

    def each(count, body):
        lax.fori_loop(0, count, lambda j, c: (body(j), c)[1], 0)

    each(PIECES, lambda j: [c.start() for c in load(j)])

    barrier = pltpu.get_barrier_semaphore()

    def greet(*targets):
        for target in targets:
            pl.semaphore_signal(barrier, inc=1, device_id=target, device_id_type=MESH)

    greet(inner_id)

    @pl.when(inside)
    def _():
        greet(rep_id, outer_id)

    @pl.when(edge)
    def _():
        greet(near_id, far_id, beyond_id, source_id)

    def prepare(part):
        for k in range(PREPARE):
            for c in load(part * PREPARE + k):
                c.wait()
        at = pl.ds(pl.multiple_of(part * PREPARE * pr, PREPARE * pr), PREPARE * pr)
        for a in range(2):
            values = raw[a, at, :].astype(jnp.float32)
            inverse = lax.rsqrt(jnp.sum(values * values, axis=1, keepdims=True) + 1e-06)
            own[a, at, :] = (values * inverse).astype(jnp.bfloat16)
            inv[a, at, :] = inverse

    def stays(j):
        return inside & jnp.logical_not(behind & (j >= PIECES - SHIFTED))

    def send_first(j):
        @pl.when(stays(j))
        def _():
            to_rep(j).start()

        @pl.when(edge)
        def _():
            to_near(j).start()

    def send_second(j):
        @pl.when(stays(j))
        def _():
            to_outer(j).start()

        @pl.when(edge)
        def _():
            to_far(j).start()

    prepare(0)

    @pl.when(inside)
    def _():
        pl.semaphore_wait(barrier, 3)

    @pl.when(edge)
    def _():
        pl.semaphore_wait(barrier, 5)

    def begin(part):
        @pl.when(part > 0)
        def _():
            prepare(part)

        for k in range(PREPARE):
            j = part * PREPARE + k

            @pl.when(j < SEND_AHEAD)
            def _():
                send_first(j)
                send_second(j)

            to_inner(j).start()

    each(PIECES // PREPARE, begin)

    def shifted(body):
        lax.fori_loop(PIECES - SHIFTED, PIECES, lambda j, c: (body(j), c)[1], 0)

    @pl.when(behind)
    def _():
        shifted(lambda j: to_outer(j).start())

    scale = jnp.exp(jnp.full((1, 1), exp_ref[0], jnp.float32))
    icpt = jnp.full((1, 1), icpt_ref[0], jnp.float32)

    def weights(side, others, diagonal):
        product = lax.dot_general(
            own[side], others, (((1,), (1,)), ((), ())), preferred_element_type=jnp.float32
        )
        logits = scale * product + icpt
        if diagonal is None:
            factor = scale / (1.0 + jnp.exp(-logits))
        else:
            row = lax.broadcasted_iota(jnp.int32, product.shape, 0)
            col = lax.broadcasted_iota(jnp.int32, product.shape, 1) + diagonal
            agree = row == col
            factor = jnp.where(agree, -scale, scale) / (1.0 + jnp.exp(jnp.where(agree, logits, -logits)))
        return factor.astype(jnp.bfloat16)

    def step(caps, imgs, diagonal=None, first=False):
        factors = [weights(1, caps, diagonal), weights(0, imgs, diagonal)]
        for side, others, factor in ((1, caps, factors[0]), (0, imgs, factors[1])):
            term = lax.dot_general(factor, others, (((1,), (0,)), ((), ())), preferred_element_type=jnp.float32)
            acc[side] = term if first else acc[side] + term

    def hand_on(j):
        @pl.when(edge)
        def _():
            turn = lax.rem(j, 2) == rep
            got_relay(0, j)

            @pl.when(turn)
            def _():
                near_across(j).start()

            near_beyond(j).start()
            got_relay(1, j)

            @pl.when(turn)
            def _():
                far_across(j).start()

            far_beyond(j).start()

    def serve(j):
        @pl.when(j + SEND_AHEAD < PIECES)
        def _():
            send_first(j + SEND_AHEAD)
            send_second(j + SEND_AHEAD)

        @pl.when(j + RELAY_AHEAD < PIECES)
        def _():
            hand_on(j + RELAY_AHEAD)

        got(REP, j)
        pass_inner(j).start()

        @pl.when(stays(j))
        def _():
            pass_outer(j).start()

    def turn_out(j):
        got(OUT_NEAR, j)
        shift_rep(j).start()

    def turn_back(j):
        got(OUT_FAR, j)
        shift_back(j).start()

    def finish(j):
        @pl.when(jnp.logical_not(beside & (j >= PIECES - SHIFTED)))
        def _():
            got(OUT_NEAR, j)
            got(OUT_FAR, j)

        got(IN_FAR, j)
        step(win[j, 0], win[j, 1])

    half = rows // 2
    for k in range(RELAY_AHEAD):
        hand_on(k)
        if k < 2:
            step(own[0, k * half:(k + 1) * half], own[1, k * half:(k + 1) * half], k * half, k == 0)

    each(PIECES, lambda j: pltpu.make_async_copy(
        pdir.at[:, rows_of(j)], pdir.at[:, rows_of(j)], pdir_recv.at[j]).wait())

    def body(j):
        @pl.when(j < PIECES)
        def _():
            serve(j)

        @pl.when(beside & (j == SHIFT_OUT))
        def _():
            shifted(turn_out)

        @pl.when(beside & (j == SHIFT_BACK))
        def _():
            shifted(turn_back)

        @pl.when(j < 2)
        def _():
            at = pl.ds(pl.multiple_of(j * half, half), half)
            step(pdir[0, at, :], pdir[1, at, :])

        @pl.when(j > 0)
        def _():
            finish(j - 1)

    each(PIECES + 1, body)

    def leave(a, out, part):
        at = pl.ds(pl.multiple_of(part * CLOSE, CLOSE), CLOSE)
        return pltpu.make_async_copy(res.at[a, at], out.at[at], out_sem.at[a, part])

    def close(a, out):
        def part(k):
            at = pl.ds(pl.multiple_of(k * CLOSE, CLOSE), CLOSE)
            direction = raw[a, at, :].astype(jnp.float32) * inv[a, at, :]
            upstream = acc[a, at, :]
            along = jnp.sum(upstream * direction, axis=1, keepdims=True)
            out[at, :] = (inv[a, at, :] * (upstream - direction * along)).astype(jnp.bfloat16)
        each(rows // CLOSE, part)

    close(1, gi_hbm)
    close(0, gc_hbm)

    def drain(j):
        to_inner(j).wait_send()
        pass_inner(j).wait_send()

        @pl.when(inside)
        def _():
            to_outer(j).wait_send()

        @pl.when(stays(j))
        def _():
            to_rep(j).wait_send()
            pass_outer(j).wait_send()

        @pl.when(beside & (j >= PIECES - SHIFTED))
        def _():
            shift_rep(j).wait_send()
            shift_back(j).wait_send()

        @pl.when(edge)
        def _():
            to_near(j).wait_send()
            to_far(j).wait_send()
            near_beyond(j).wait_send()
            far_beyond(j).wait_send()

            @pl.when(lax.rem(j, 2) == rep)
            def _():
                near_across(j).wait_send()
                far_across(j).wait_send()

    each(PIECES, drain)


def solution(mesh):
    n_blk = mesh.shape["blk"]

    def shards(photo_vectors, caption_vectors, exponent_of_scale, additive_intercept):
        rows, width = photo_vectors.shape
        pr = rows // PIECES
        bf16, f32 = jnp.bfloat16, jnp.float32
        dma = pltpu.SemaphoreType.DMA
        vmem = pl.BlockSpec(memory_space=pltpu.VMEM)
        smem = pl.BlockSpec(memory_space=pltpu.SMEM)
        anywhere = pl.BlockSpec(memory_space=pl.ANY)
        return pl.pallas_call(
            functools.partial(kernel, n_blk, 8),
            out_shape=[pltpu.VMEM((rows, width), bf16)] * 2,
            in_specs=[smem, smem, anywhere, anywhere],
            out_specs=[vmem] * 2,
            scratch_shapes=[
                pltpu.VMEM((2, rows, width), bf16),
                pltpu.VMEM((2, rows, 1), f32),
                pltpu.VMEM((2, rows, width), bf16),
                pltpu.VMEM((2, rows, width), bf16),
                pltpu.VMEM((PIECES, 2, 4 * pr, width), bf16),
                pltpu.VMEM((2, 2, rows, width), bf16),
                pltpu.VMEM((2, rows, width), f32),
                pltpu.VMEM((2, rows, width), bf16),
                dma((2, PIECES)),
                dma((2, PIECES)),
                dma((4, PIECES)),
                dma((PIECES,)),
                dma((2, PIECES)),
            ] + [dma((PIECES,))] * 7 + [dma((2, PIECES)), dma((PIECES,)), dma((PIECES,))],
            compiler_params=pltpu.CompilerParams(
                collective_id=0, has_side_effects=True, vmem_limit_bytes=56 * 1024 * 1024
            ),
            cost_estimate=pl.CostEstimate(
                flops=24 * 2 * rows * rows * width, bytes_accessed=8 * rows * width, transcendentals=12 * rows * rows
            ),
        )(
            exponent_of_scale, additive_intercept, photo_vectors, caption_vectors
        )

    whole = P(("blk", "rep"), None)
    return jax.shard_map(
        shards,
        mesh=mesh,
        in_specs=(whole, whole, P(), P()),
        out_specs=(whole, whole),
        check_vma=False,
    )
```

```python
import functools

import jax
import jax.numpy as jnp
from jax import lax
from jax.experimental import pallas as pl
from jax.experimental.pallas import tpu as pltpu
from jax.sharding import PartitionSpec as P

MESH = pl.DeviceIdType.MESH
PIECES = 8
EDGE_AHEAD = 4
BEHIND_AHEAD = 1
REP_AHEAD = 2
OUT_AHEAD = 2
RELAY_AHEAD = 2
SHIFTED = 2
SHIFT_OUT = 1
SHIFT_BACK = 3
PREPARE = 2
CLOSE = 256
OUT_NEAR, REP, IN_FAR, OUT_FAR = range(4)


def kernel(
    n_blk, n_z, exp_ref, icpt_ref, img_hbm, cap_hbm, gi_hbm, gc_hbm,
    raw, inv, own, pdir, win, relay, acc, res,
    raw_sem, out_sem, win_recv, pdir_recv, relay_recv,
    in_send, rep_send, out_send, fin_send, fout_send, near_send, far_send, cross_send, shift_send, back_send,
):
    rows, width = own.shape[1], own.shape[2]
    pr = rows // PIECES
    blk, rep = lax.axis_index("blk"), lax.axis_index("rep")
    core = lax.rem(blk, 2)
    z = lax.rem(blk // 2, n_z)
    away = 2 * core - 1
    outer = lax.rem(blk + away + n_blk, n_blk)
    inner = blk - away
    edge = z == core * (n_z - 1)
    inside = jnp.logical_not(edge)
    behind = z == (1 - core) * (n_z - 1)
    beside = z == core * (n_z - 2) + (1 - core)
    pal = blk + 2 * n_z * (1 - 2 * lax.rem(blk // (2 * n_z), 2))
    beyond = lax.rem(pal + away + n_blk, n_blk)
    outer_low = lax.rem(outer // (2 * n_z), 2)
    source = outer + 2 * n_z * (1 - 2 * outer_low)
    first_ahead = jnp.where(edge, EDGE_AHEAD, jnp.where(behind, BEHIND_AHEAD, REP_AHEAD))
    second_ahead = jnp.where(edge, EDGE_AHEAD, OUT_AHEAD)
    rep_id = {"blk": blk, "rep": 1 - rep}
    inner_id = {"blk": inner, "rep": rep}
    outer_id = {"blk": outer, "rep": rep}
    near_id = {"blk": pal, "rep": rep}
    far_id = {"blk": pal, "rep": 1 - rep}
    beyond_id = {"blk": beyond, "rep": rep}
    source_id = {"blk": source, "rep": rep}

    def rows_of(j):
        return pl.ds(pl.multiple_of(j * pr, pr), pr)

    def load(j):
        return (
            pltpu.make_async_copy(cap_hbm.at[rows_of(j)], raw.at[0, rows_of(j)], raw_sem.at[0, j]),
            pltpu.make_async_copy(img_hbm.at[rows_of(j)], raw.at[1, rows_of(j)], raw_sem.at[1, j]),
        )

    def slot(place, j):
        return win.at[j, :, pl.ds(place * pr, pr)]

    def remote(src, dst, send, recv, target):
        return pltpu.make_async_remote_copy(
            src_ref=src, dst_ref=dst, send_sem=send, recv_sem=recv, device_id=target, device_id_type=MESH
        )

    def mine(j):
        return own.at[:, rows_of(j)]

    def to_rep(j):
        return remote(mine(j), slot(REP, j), rep_send.at[j], win_recv.at[REP, j], rep_id)

    def to_outer(j):
        return remote(mine(j), slot(OUT_NEAR, j), out_send.at[j], win_recv.at[OUT_NEAR, j], outer_id)

    def to_inner(j):
        return remote(mine(j), pdir.at[:, rows_of(j)], in_send.at[j], pdir_recv.at[j], inner_id)

    def to_near(j):
        return remote(mine(j), relay.at[0, :, rows_of(j)], rep_send.at[j], relay_recv.at[0, j], near_id)

    def to_far(j):
        return remote(mine(j), relay.at[1, :, rows_of(j)], out_send.at[j], relay_recv.at[1, j], far_id)

    def pass_inner(j):
        return remote(slot(REP, j), slot(IN_FAR, j), fin_send.at[j], win_recv.at[IN_FAR, j], inner_id)

    def pass_outer(j):
        return remote(slot(REP, j), slot(OUT_FAR, j), fout_send.at[j], win_recv.at[OUT_FAR, j], outer_id)

    def shift_rep(j):
        return remote(slot(OUT_NEAR, j), slot(OUT_FAR, j), shift_send.at[j], win_recv.at[OUT_FAR, j], rep_id)

    def shift_back(j):
        return remote(slot(OUT_FAR, j), slot(REP, j), back_send.at[j], win_recv.at[REP, j], outer_id)

    def near_beyond(j):
        return remote(relay.at[0, :, rows_of(j)], slot(OUT_NEAR, j), near_send.at[j], win_recv.at[OUT_NEAR, j], beyond_id)

    def far_beyond(j):
        return remote(relay.at[1, :, rows_of(j)], slot(OUT_FAR, j), far_send.at[j], win_recv.at[OUT_FAR, j], beyond_id)

    def near_across(j):
        return remote(relay.at[0, :, rows_of(j)], slot(REP, j), cross_send.at[0, j], win_recv.at[REP, j], far_id)

    def far_across(j):
        return remote(relay.at[1, :, rows_of(j)], slot(REP, j), cross_send.at[1, j], win_recv.at[REP, j], near_id)

    def got(place, j):
        pltpu.make_async_copy(slot(place, j), slot(place, j), win_recv.at[place, j]).wait()

    def got_relay(side, j):
        at = relay.at[side, :, rows_of(j)]
        pltpu.make_async_copy(at, at, relay_recv.at[side, j]).wait()

    def each(count, body):
        lax.fori_loop(0, count, lambda j, c: (body(j), c)[1], 0)

    each(PIECES, lambda j: [c.start() for c in load(j)])

    barrier = pltpu.get_barrier_semaphore()

    def greet(*targets):
        for target in targets:
            pl.semaphore_signal(barrier, inc=1, device_id=target, device_id_type=MESH)

    greet(inner_id)

    @pl.when(inside)
    def _():
        greet(rep_id, outer_id)

    @pl.when(edge)
    def _():
        greet(near_id, far_id, beyond_id, source_id)

    def prepare(part):
        for k in range(PREPARE):
            for c in load(part * PREPARE + k):
                c.wait()
        at = pl.ds(pl.multiple_of(part * PREPARE * pr, PREPARE * pr), PREPARE * pr)
        for a in range(2):
            values = raw[a, at, :].astype(jnp.float32)
            inverse = lax.rsqrt(jnp.sum(values * values, axis=1, keepdims=True) + 1e-06)
            own[a, at, :] = (values * inverse).astype(jnp.bfloat16)
            inv[a, at, :] = inverse

    def stays(j):
        return inside & jnp.logical_not(behind & (j >= PIECES - SHIFTED))

    def send_first(j):
        @pl.when(stays(j))
        def _():
            to_rep(j).start()

        @pl.when(edge)
        def _():
            to_near(j).start()

    def send_second(j):
        @pl.when(stays(j))
        def _():
            to_outer(j).start()

        @pl.when(edge)
        def _():
            to_far(j).start()

    prepare(0)

    @pl.when(inside)
    def _():
        pl.semaphore_wait(barrier, 3)

    @pl.when(edge)
    def _():
        pl.semaphore_wait(barrier, 5)

    def begin(part):
        @pl.when(part > 0)
        def _():
            prepare(part)

        for k in range(PREPARE):
            j = part * PREPARE + k

            @pl.when(j < first_ahead)
            def _():
                send_first(j)

            @pl.when(j < second_ahead)
            def _():
                send_second(j)

            to_inner(j).start()

    each(PIECES // PREPARE, begin)

    def shifted(body):
        lax.fori_loop(PIECES - SHIFTED, PIECES, lambda j, c: (body(j), c)[1], 0)

    @pl.when(behind)
    def _():
        shifted(lambda j: to_outer(j).start())

    scale = jnp.exp(jnp.full((1, 1), exp_ref[0], jnp.float32))
    icpt = jnp.full((1, 1), icpt_ref[0], jnp.float32)

    def weights(side, others, diagonal):
        product = lax.dot_general(
            own[side], others, (((1,), (1,)), ((), ())), preferred_element_type=jnp.float32
        )
        logits = scale * product + icpt
        if diagonal is None:
            factor = scale / (1.0 + jnp.exp(-logits))
        else:
            row = lax.broadcasted_iota(jnp.int32, product.shape, 0)
            col = lax.broadcasted_iota(jnp.int32, product.shape, 1) + diagonal
            agree = row == col
            factor = jnp.where(agree, -scale, scale) / (1.0 + jnp.exp(jnp.where(agree, logits, -logits)))
        return factor.astype(jnp.bfloat16)

    def step(caps, imgs, diagonal=None, first=False):
        factors = [weights(1, caps, diagonal), weights(0, imgs, diagonal)]
        for side, others, factor in ((1, caps, factors[0]), (0, imgs, factors[1])):
            term = lax.dot_general(factor, others, (((1,), (0,)), ((), ())), preferred_element_type=jnp.float32)
            acc[side] = term if first else acc[side] + term

    def hand_on(j):
        @pl.when(edge)
        def _():
            turn = lax.rem(j, 2) == rep
            got_relay(0, j)

            @pl.when(turn)
            def _():
                near_across(j).start()

            near_beyond(j).start()
            got_relay(1, j)

            @pl.when(turn)
            def _():
                far_across(j).start()

            far_beyond(j).start()

    def serve(j):
        @pl.when(j + first_ahead < PIECES)
        def _():
            send_first(j + first_ahead)

        @pl.when(j + second_ahead < PIECES)
        def _():
            send_second(j + second_ahead)

        @pl.when(j + RELAY_AHEAD < PIECES)
        def _():
            hand_on(j + RELAY_AHEAD)

        got(REP, j)
        pass_inner(j).start()

        @pl.when(stays(j))
        def _():
            pass_outer(j).start()

    def turn_out(j):
        got(OUT_NEAR, j)
        shift_rep(j).start()

    def turn_back(j):
        got(OUT_FAR, j)
        shift_back(j).start()

    def finish(j):
        @pl.when(jnp.logical_not(beside & (j >= PIECES - SHIFTED)))
        def _():
            got(OUT_NEAR, j)
            got(OUT_FAR, j)

        got(IN_FAR, j)
        step(win[j, 0], win[j, 1])

    half = rows // 2
    for k in range(RELAY_AHEAD):
        hand_on(k)
        if k < 2:
            step(own[0, k * half:(k + 1) * half], own[1, k * half:(k + 1) * half], k * half, k == 0)

    each(PIECES, lambda j: pltpu.make_async_copy(
        pdir.at[:, rows_of(j)], pdir.at[:, rows_of(j)], pdir_recv.at[j]).wait())

    def body(j):
        @pl.when(j < PIECES)
        def _():
            serve(j)

        @pl.when(beside & (j == SHIFT_OUT))
        def _():
            shifted(turn_out)

        @pl.when(beside & (j == SHIFT_BACK))
        def _():
            shifted(turn_back)

        @pl.when(j < 2)
        def _():
            at = pl.ds(pl.multiple_of(j * half, half), half)
            step(pdir[0, at, :], pdir[1, at, :])

        @pl.when(j > 0)
        def _():
            finish(j - 1)

    each(PIECES + 1, body)

    def leave(a, out, part):
        at = pl.ds(pl.multiple_of(part * CLOSE, CLOSE), CLOSE)
        return pltpu.make_async_copy(res.at[a, at], out.at[at], out_sem.at[a, part])

    def close(a, out):
        def part(k):
            at = pl.ds(pl.multiple_of(k * CLOSE, CLOSE), CLOSE)
            direction = raw[a, at, :].astype(jnp.float32) * inv[a, at, :]
            upstream = acc[a, at, :]
            along = jnp.sum(upstream * direction, axis=1, keepdims=True)
            out[at, :] = (inv[a, at, :] * (upstream - direction * along)).astype(jnp.bfloat16)
        each(rows // CLOSE, part)

    close(1, gi_hbm)
    close(0, gc_hbm)

    def drain(j):
        to_inner(j).wait_send()
        pass_inner(j).wait_send()

        @pl.when(inside)
        def _():
            to_outer(j).wait_send()

        @pl.when(stays(j))
        def _():
            to_rep(j).wait_send()
            pass_outer(j).wait_send()

        @pl.when(beside & (j >= PIECES - SHIFTED))
        def _():
            shift_rep(j).wait_send()
            shift_back(j).wait_send()

        @pl.when(edge)
        def _():
            to_near(j).wait_send()
            to_far(j).wait_send()
            near_beyond(j).wait_send()
            far_beyond(j).wait_send()

            @pl.when(lax.rem(j, 2) == rep)
            def _():
                near_across(j).wait_send()
                far_across(j).wait_send()

    each(PIECES, drain)


def solution(mesh):
    n_blk = mesh.shape["blk"]

    def shards(photo_vectors, caption_vectors, exponent_of_scale, additive_intercept):
        rows, width = photo_vectors.shape
        pr = rows // PIECES
        bf16, f32 = jnp.bfloat16, jnp.float32
        dma = pltpu.SemaphoreType.DMA
        vmem = pl.BlockSpec(memory_space=pltpu.VMEM)
        smem = pl.BlockSpec(memory_space=pltpu.SMEM)
        anywhere = pl.BlockSpec(memory_space=pl.ANY)
        return pl.pallas_call(
            functools.partial(kernel, n_blk, 8),
            out_shape=[pltpu.VMEM((rows, width), bf16)] * 2,
            in_specs=[smem, smem, anywhere, anywhere],
            out_specs=[vmem] * 2,
            scratch_shapes=[
                pltpu.VMEM((2, rows, width), bf16),
                pltpu.VMEM((2, rows, 1), f32),
                pltpu.VMEM((2, rows, width), bf16),
                pltpu.VMEM((2, rows, width), bf16),
                pltpu.VMEM((PIECES, 2, 4 * pr, width), bf16),
                pltpu.VMEM((2, 2, rows, width), bf16),
                pltpu.VMEM((2, rows, width), f32),
                pltpu.VMEM((2, rows, width), bf16),
                dma((2, PIECES)),
                dma((2, PIECES)),
                dma((4, PIECES)),
                dma((PIECES,)),
                dma((2, PIECES)),
            ] + [dma((PIECES,))] * 7 + [dma((2, PIECES)), dma((PIECES,)), dma((PIECES,))],
            compiler_params=pltpu.CompilerParams(
                collective_id=0, has_side_effects=True, vmem_limit_bytes=56 * 1024 * 1024
            ),
            cost_estimate=pl.CostEstimate(
                flops=24 * 2 * rows * rows * width, bytes_accessed=8 * rows * width, transcendentals=12 * rows * rows
            ),
        )(
            exponent_of_scale, additive_intercept, photo_vectors, caption_vectors
        )

    whole = P(("blk", "rep"), None)
    return jax.shard_map(
        shards,
        mesh=mesh,
        in_specs=(whole, whole, P(), P()),
        out_specs=(whole, whole),
        check_vma=False,
    )
```

```python
import functools

import jax
import jax.numpy as jnp
from jax import lax
from jax.experimental import pallas as pl
from jax.experimental.pallas import tpu as pltpu
from jax.sharding import PartitionSpec as P

MESH = pl.DeviceIdType.MESH
PIECES = 8
EDGE_AHEAD = 4
BEHIND_AHEAD = 1
REP_AHEAD = 2
OUT_AHEAD = 2
BESIDE_AHEAD = 3
RELAY_AHEAD = 2
SETTLED = 3
SHIFTED = 2
SHIFT_OUT = 1
SHIFT_BACK = 3
PREPARE = 2
CLOSE = 256
OUT_NEAR, REP, IN_FAR, OUT_FAR = range(4)


def kernel(
    n_blk, n_z, exp_ref, icpt_ref, img_hbm, cap_hbm, gi_hbm, gc_hbm,
    raw, inv, own, pdir, win, relay, acc, res,
    raw_sem, out_sem, win_recv, pdir_recv, relay_recv,
    in_send, rep_send, out_send, fin_send, fout_send, near_send, far_send, cross_send, shift_send, back_send,
):
    rows, width = own.shape[1], own.shape[2]
    pr = rows // PIECES
    blk, rep = lax.axis_index("blk"), lax.axis_index("rep")
    core = lax.rem(blk, 2)
    z = lax.rem(blk // 2, n_z)
    away = 2 * core - 1
    outer = lax.rem(blk + away + n_blk, n_blk)
    inner = blk - away
    edge = z == core * (n_z - 1)
    inside = jnp.logical_not(edge)
    behind = z == (1 - core) * (n_z - 1)
    beside = z == core * (n_z - 2) + (1 - core)
    pal = blk + 2 * n_z * (1 - 2 * lax.rem(blk // (2 * n_z), 2))
    beyond = lax.rem(pal + away + n_blk, n_blk)
    outer_low = lax.rem(outer // (2 * n_z), 2)
    source = outer + 2 * n_z * (1 - 2 * outer_low)
    first_ahead = jnp.where(edge, EDGE_AHEAD, jnp.where(behind, BEHIND_AHEAD, REP_AHEAD))
    second_ahead = jnp.where(edge, EDGE_AHEAD, jnp.where(beside, BESIDE_AHEAD, OUT_AHEAD))
    rep_id = {"blk": blk, "rep": 1 - rep}
    inner_id = {"blk": inner, "rep": rep}
    outer_id = {"blk": outer, "rep": rep}
    near_id = {"blk": pal, "rep": rep}
    far_id = {"blk": pal, "rep": 1 - rep}
    beyond_id = {"blk": beyond, "rep": rep}
    source_id = {"blk": source, "rep": rep}

    def rows_of(j):
        return pl.ds(pl.multiple_of(j * pr, pr), pr)

    def load(j):
        return (
            pltpu.make_async_copy(cap_hbm.at[rows_of(j)], raw.at[0, rows_of(j)], raw_sem.at[0, j]),
            pltpu.make_async_copy(img_hbm.at[rows_of(j)], raw.at[1, rows_of(j)], raw_sem.at[1, j]),
        )

    def slot(place, j):
        return win.at[j, :, pl.ds(place * pr, pr)]

    def remote(src, dst, send, recv, target):
        return pltpu.make_async_remote_copy(
            src_ref=src, dst_ref=dst, send_sem=send, recv_sem=recv, device_id=target, device_id_type=MESH
        )

    def mine(j):
        return own.at[:, rows_of(j)]

    def to_rep(j):
        return remote(mine(j), slot(REP, j), rep_send.at[j], win_recv.at[REP, j], rep_id)

    def to_outer(j):
        return remote(mine(j), slot(OUT_NEAR, j), out_send.at[j], win_recv.at[OUT_NEAR, j], outer_id)

    def to_inner(j):
        return remote(mine(j), pdir.at[:, rows_of(j)], in_send.at[j], pdir_recv.at[j], inner_id)

    def to_near(j):
        return remote(mine(j), relay.at[0, :, rows_of(j)], rep_send.at[j], relay_recv.at[0, j], near_id)

    def to_far(j):
        return remote(mine(j), relay.at[1, :, rows_of(j)], out_send.at[j], relay_recv.at[1, j], far_id)

    def pass_inner(j):
        return remote(slot(REP, j), slot(IN_FAR, j), fin_send.at[j], win_recv.at[IN_FAR, j], inner_id)

    def pass_outer(j):
        return remote(slot(REP, j), slot(OUT_FAR, j), fout_send.at[j], win_recv.at[OUT_FAR, j], outer_id)

    def shift_rep(j):
        return remote(slot(OUT_NEAR, j), slot(OUT_FAR, j), shift_send.at[j], win_recv.at[OUT_FAR, j], rep_id)

    def shift_back(j):
        return remote(slot(OUT_FAR, j), slot(REP, j), back_send.at[j], win_recv.at[REP, j], outer_id)

    def near_beyond(j):
        return remote(relay.at[0, :, rows_of(j)], slot(OUT_NEAR, j), near_send.at[j], win_recv.at[OUT_NEAR, j], beyond_id)

    def far_beyond(j):
        return remote(relay.at[1, :, rows_of(j)], slot(OUT_FAR, j), far_send.at[j], win_recv.at[OUT_FAR, j], beyond_id)

    def near_across(j):
        return remote(relay.at[0, :, rows_of(j)], slot(REP, j), cross_send.at[0, j], win_recv.at[REP, j], far_id)

    def far_across(j):
        return remote(relay.at[1, :, rows_of(j)], slot(REP, j), cross_send.at[1, j], win_recv.at[REP, j], near_id)

    def got(place, j):
        pltpu.make_async_copy(slot(place, j), slot(place, j), win_recv.at[place, j]).wait()

    def got_relay(side, j):
        at = relay.at[side, :, rows_of(j)]
        pltpu.make_async_copy(at, at, relay_recv.at[side, j]).wait()

    def each(count, body):
        lax.fori_loop(0, count, lambda j, c: (body(j), c)[1], 0)

    each(PIECES, lambda j: [c.start() for c in load(j)])

    barrier = pltpu.get_barrier_semaphore()

    def greet(*targets):
        for target in targets:
            pl.semaphore_signal(barrier, inc=1, device_id=target, device_id_type=MESH)

    greet(inner_id)

    @pl.when(inside)
    def _():
        greet(rep_id, outer_id)

    @pl.when(edge)
    def _():
        greet(near_id, far_id, beyond_id, source_id)

    def prepare(part):
        for k in range(PREPARE):
            for c in load(part * PREPARE + k):
                c.wait()
        at = pl.ds(pl.multiple_of(part * PREPARE * pr, PREPARE * pr), PREPARE * pr)
        for a in range(2):
            values = raw[a, at, :].astype(jnp.float32)
            inverse = lax.rsqrt(jnp.sum(values * values, axis=1, keepdims=True) + 1e-06)
            own[a, at, :] = (values * inverse).astype(jnp.bfloat16)
            inv[a, at, :] = inverse

    def stays(j):
        return inside & jnp.logical_not(behind & (j >= PIECES - SHIFTED))

    def send_first(j):
        @pl.when(stays(j))
        def _():
            to_rep(j).start()

        @pl.when(edge)
        def _():
            to_near(j).start()

    def send_second(j):
        @pl.when(stays(j))
        def _():
            to_outer(j).start()

        @pl.when(edge)
        def _():
            to_far(j).start()

    prepare(0)

    @pl.when(inside)
    def _():
        pl.semaphore_wait(barrier, 3)

    @pl.when(edge)
    def _():
        pl.semaphore_wait(barrier, 5)

    def begin(part):
        @pl.when(part > 0)
        def _():
            prepare(part)

        for k in range(PREPARE):
            j = part * PREPARE + k

            @pl.when(j < first_ahead)
            def _():
                send_first(j)

            @pl.when(j < second_ahead)
            def _():
                send_second(j)

            to_inner(j).start()

    each(PIECES // PREPARE, begin)

    def shifted(body):
        lax.fori_loop(PIECES - SHIFTED, PIECES, lambda j, c: (body(j), c)[1], 0)

    @pl.when(behind)
    def _():
        shifted(lambda j: to_outer(j).start())

    scale = jnp.exp(jnp.full((1, 1), exp_ref[0], jnp.float32))
    icpt = jnp.full((1, 1), icpt_ref[0], jnp.float32)

    def weights(side, others, diagonal):
        product = lax.dot_general(
            own[side], others, (((1,), (1,)), ((), ())), preferred_element_type=jnp.float32
        )
        logits = scale * product + icpt
        if diagonal is None:
            factor = scale / (1.0 + jnp.exp(-logits))
        else:
            row = lax.broadcasted_iota(jnp.int32, product.shape, 0)
            col = lax.broadcasted_iota(jnp.int32, product.shape, 1) + diagonal
            agree = row == col
            factor = jnp.where(agree, -scale, scale) / (1.0 + jnp.exp(jnp.where(agree, logits, -logits)))
        return factor.astype(jnp.bfloat16)

    def step(caps, imgs, diagonal=None, first=False):
        factors = [weights(1, caps, diagonal), weights(0, imgs, diagonal)]
        for side, others, factor in ((1, caps, factors[0]), (0, imgs, factors[1])):
            term = lax.dot_general(factor, others, (((1,), (0,)), ((), ())), preferred_element_type=jnp.float32)
            acc[side] = term if first else acc[side] + term

    def hand_on(j):
        @pl.when(edge)
        def _():
            turn = lax.rem(j, 2) == rep
            got_relay(0, j)

            near_beyond(j).start()

            @pl.when(turn)
            def _():
                near_across(j).start()

            got_relay(1, j)

            far_beyond(j).start()

            @pl.when(turn)
            def _():
                far_across(j).start()


    def serve(j):
        @pl.when(j + first_ahead < PIECES)
        def _():
            send_first(j + first_ahead)

        @pl.when(j + second_ahead < PIECES)
        def _():
            send_second(j + second_ahead)

        @pl.when(j + RELAY_AHEAD < PIECES)
        def _():
            hand_on(j + RELAY_AHEAD)

        got(REP, j)
        pass_inner(j).start()

        @pl.when(stays(j))
        def _():
            pass_outer(j).start()

    def turn_out(j):
        got(OUT_NEAR, j)
        shift_rep(j).start()

    def turn_back(j):
        got(OUT_FAR, j)
        shift_back(j).start()

    def finish(j):
        @pl.when(jnp.logical_not(beside & (j >= PIECES - SHIFTED)))
        def _():
            got(OUT_NEAR, j)
            got(OUT_FAR, j)

        got(IN_FAR, j)
        step(win[j, 0], win[j, 1])

    half = rows // 2
    each(RELAY_AHEAD, hand_on)
    for k in range(2):
        step(own[0, k * half:(k + 1) * half], own[1, k * half:(k + 1) * half], k * half, k == 0)

    each(PIECES, lambda j: pltpu.make_async_copy(
        pdir.at[:, rows_of(j)], pdir.at[:, rows_of(j)], pdir_recv.at[j]).wait())

    def drain(j):
        to_inner(j).wait_send()
        pass_inner(j).wait_send()

        @pl.when(inside)
        def _():
            to_outer(j).wait_send()

        @pl.when(stays(j))
        def _():
            to_rep(j).wait_send()
            pass_outer(j).wait_send()

        @pl.when(beside & (j >= PIECES - SHIFTED))
        def _():
            shift_rep(j).wait_send()
            shift_back(j).wait_send()

        @pl.when(edge)
        def _():
            to_near(j).wait_send()
            to_far(j).wait_send()
            near_beyond(j).wait_send()
            far_beyond(j).wait_send()

            @pl.when(lax.rem(j, 2) == rep)
            def _():
                near_across(j).wait_send()
                far_across(j).wait_send()

    def body(j):
        @pl.when(j < PIECES)
        def _():
            serve(j)

        @pl.when(beside & (j == SHIFT_OUT))
        def _():
            shifted(turn_out)

        @pl.when(beside & (j == SHIFT_BACK))
        def _():
            shifted(turn_back)

        @pl.when(j < 2)
        def _():
            at = pl.ds(pl.multiple_of(j * half, half), half)
            step(pdir[0, at, :], pdir[1, at, :])

        @pl.when(j > SETTLED)
        def _():
            drain(j - 1 - SETTLED)

        @pl.when(j > 0)
        def _():
            finish(j - 1)

    each(PIECES + 1, body)
    lax.fori_loop(PIECES - SETTLED, PIECES, lambda j, c: (drain(j), c)[1], 0)

    def leave(a, out, part):
        at = pl.ds(pl.multiple_of(part * CLOSE, CLOSE), CLOSE)
        return pltpu.make_async_copy(res.at[a, at], out.at[at], out_sem.at[a, part])

    def close(a, out):
        def part(k):
            at = pl.ds(pl.multiple_of(k * CLOSE, CLOSE), CLOSE)
            direction = raw[a, at, :].astype(jnp.float32) * inv[a, at, :]
            upstream = acc[a, at, :]
            along = jnp.sum(upstream * direction, axis=1, keepdims=True)
            out[at, :] = (inv[a, at, :] * (upstream - direction * along)).astype(jnp.bfloat16)
        each(rows // CLOSE, part)

    close(1, gi_hbm)
    close(0, gc_hbm)


def solution(mesh):
    n_blk = mesh.shape["blk"]

    def shards(photo_vectors, caption_vectors, exponent_of_scale, additive_intercept):
        rows, width = photo_vectors.shape
        pr = rows // PIECES
        bf16, f32 = jnp.bfloat16, jnp.float32
        dma = pltpu.SemaphoreType.DMA
        vmem = pl.BlockSpec(memory_space=pltpu.VMEM)
        smem = pl.BlockSpec(memory_space=pltpu.SMEM)
        anywhere = pl.BlockSpec(memory_space=pl.ANY)
        return pl.pallas_call(
            functools.partial(kernel, n_blk, 8),
            out_shape=[pltpu.VMEM((rows, width), bf16)] * 2,
            in_specs=[smem, smem, anywhere, anywhere],
            out_specs=[vmem] * 2,
            scratch_shapes=[
                pltpu.VMEM((2, rows, width), bf16),
                pltpu.VMEM((2, rows, 1), f32),
                pltpu.VMEM((2, rows, width), bf16),
                pltpu.VMEM((2, rows, width), bf16),
                pltpu.VMEM((PIECES, 2, 4 * pr, width), bf16),
                pltpu.VMEM((2, 2, rows, width), bf16),
                pltpu.VMEM((2, rows, width), f32),
                pltpu.VMEM((2, rows, width), bf16),
                dma((2, PIECES)),
                dma((2, PIECES)),
                dma((4, PIECES)),
                dma((PIECES,)),
                dma((2, PIECES)),
            ] + [dma((PIECES,))] * 7 + [dma((2, PIECES)), dma((PIECES,)), dma((PIECES,))],
            compiler_params=pltpu.CompilerParams(
                collective_id=0, has_side_effects=True, vmem_limit_bytes=56 * 1024 * 1024
            ),
            cost_estimate=pl.CostEstimate(
                flops=24 * 2 * rows * rows * width, bytes_accessed=8 * rows * width, transcendentals=12 * rows * rows
            ),
        )(
            exponent_of_scale, additive_intercept, photo_vectors, caption_vectors
        )

    whole = P(("blk", "rep"), None)
    return jax.shard_map(
        shards,
        mesh=mesh,
        in_specs=(whole, whole, P(), P()),
        out_specs=(whole, whole),
        check_vma=False,
    )
```
